32 devices in a mesh: groups: 2 (over x), dp: 16 (over z, y, core).
Axes of the slice: x: 2, y: 2, z: 4, core: 2. Of those that a mesh axis runs over, the one named last changes fastest.
Arguments:
- states: bfloat16 [16384, 1024], P(('groups', 'dp')), parts along dimension 0, may hold values from -6 to 6
- lengths: int32 [64], P(('groups', 'dp')), parts along dimension 0, may hold values from 1 to 256, as said below
- norm_gain: bfloat16 [1024], replicated, may hold values from 0.5 to 2
- w_gate: bfloat16 [1024, 1536], replicated, may hold values from -0.1875 to 0.1875
- w_up: bfloat16 [1024, 1536], replicated, may hold values from -0.1875 to 0.1875
- w_down: bfloat16 [1536, 1024], replicated, may hold values from -0.15625 to 0.15625
- context: bfloat16 [64, 4096], P('groups', 'dp'), parts along dimension 0, may hold values from -6 to 6
- w_out: bfloat16 [4096, 4096], P('dp'), may hold values from -0.09375 to 0.09375
- resid_stream: bfloat16 [64, 4096], P('groups'), parts along dimension 0, may hold values from -6 to 6
- teacher_gain: bfloat16 [4096], replicated, may hold values from 0.5 to 2
Outputs:
- gram_loss: float32 [2], P('groups'), parts along dimension 0
- grad_gate: float32 [2048, 1536], P(('groups', 'dp')), parts along dimension 0
- grad_up: float32 [2048, 1536], P(('groups', 'dp')), parts along dimension 0
- grad_down: float32 [3072, 1024], P(('groups', 'dp')), parts along dimension 0
The draws below stay inside these ranges and needn't reach their ends.
There are 2 independent parts, one for each index of `groups`. The reference program is written for one: setup_inputs(seed, part) draws one part's arguments, and reference() takes and returns one part's arrays. A program takes and returns all parts, laid end to end along the dimension named above; an argument that names none is the same for every part. Nothing has to cross between parts.
Inputs may be any that keep to these rules, and one draw needn't show every extreme that they name: `lengths`: some document of every group fills all 256 slots and some has a single valid token.
All inputs are finite; a program needn't handle non-finite values.
Results may differ from the reference program's by a relative error of at most 0.004.
Values may be sent and summed in bfloat16 or wider, within the bound.
No kernel may reach another device: no remote copies, remote signals or barrier semaphores. Data moves between devices by JAX's collectives and lax.ppermute only.
A program may use at most 128 MiB of HBM per device.

```python
import math
import jax
import jax.numpy as jnp
from jax import lax

SD = 1024
FF = 1536
TD = 4096
SEQ = 256
DOCS = 32
TOKENS = 8192


def draw_lengths(key, part):
    drawn_lengths = jax.random.randint(key, (DOCS,), 1, SEQ + 1)
    full_index = jax.random.randint(jax.random.fold_in(key, 7), (), 0, DOCS)
    positions = jnp.arange(DOCS, dtype=jnp.int32)
    drawn_lengths = jnp.where(positions == full_index, SEQ, drawn_lengths)
    drawn_lengths = jnp.where(positions == (full_index + 1) % DOCS, 1, drawn_lengths)
    return drawn_lengths.astype(jnp.int32)


def steps_of(key, extent, shards, low, largest):
    def one(axis_at, shards_of):
        steps = jax.random.uniform(jax.random.fold_in(jax.random.fold_in(key, 6), axis_at), (shards_of,), jnp.float32, low / len(shards), largest / len(shards))
        return jnp.repeat(jnp.exp(steps), extent[axis_at] // shards_of).reshape((-1,) + (1,) * (len(extent) - axis_at - 1))

    factor_of = one(*shards[0])
    for cut in shards[1:]:
        factor_of = factor_of * one(*cut)
    return factor_of


def scatter_about(rng, extent, deviation, limit, cuts=(), held_as=jnp.bfloat16):
    entries = jax.random.normal(rng, extent, jnp.float32) * deviation
    if len(cuts) > 0:
        entries = steps_of(rng, extent, cuts, -0.22, 0.18) * entries
    return jnp.clip(entries, min=-limit, max=limit).astype(held_as)


def setup_inputs(seed: int = 0, part: int = 0) -> dict:
    splits = jax.random.split(jax.random.key(seed), 11)
    own_keys = jax.random.split(jax.random.fold_in(splits[10], part), 11)
    states = scatter_about(own_keys[0], (TOKENS, SD), 1.0, 6.0, ((0, 16),))
    lengths = draw_lengths(jax.random.fold_in(jax.random.fold_in(splits[10], part), 71), part)
    norm_gain = jnp.clip(jnp.exp(jax.random.uniform(splits[2], (SD,), jnp.float32, math.log(0.5), math.log(2.0))), 0.5, 2.0).astype(jnp.bfloat16)
    w_gate = scatter_about(splits[3], (SD, FF), SD ** -0.5, 0.1875)
    w_up = scatter_about(splits[4], (SD, FF), SD ** -0.5, 0.1875)
    w_down = scatter_about(splits[5], (FF, SD), FF ** -0.5, 0.15625)
    context = scatter_about(own_keys[6], (DOCS, TD), 1.0, 6.0, ((1, 16),))
    w_out = scatter_about(splits[7], (TD, TD), TD ** -0.5, 0.09375, ((0, 16),))
    resid_stream = scatter_about(own_keys[8], (DOCS, TD), 1.0, 6.0)
    teacher_gain = jnp.clip(jnp.exp(jax.random.uniform(splits[9], (TD,), jnp.float32, math.log(0.5), math.log(2.0))), 0.5, 2.0).astype(jnp.bfloat16)
    return dict(states=states, lengths=lengths, norm_gain=norm_gain, w_gate=w_gate, w_up=w_up, w_down=w_down, context=context, w_out=w_out, resid_stream=resid_stream, teacher_gain=teacher_gain)


EPS = 1e-06
LOSS_SCALE = 4096.0

def teacher_embed(attn_rows, resid_rows, teacher_gain):
    scaled_rows = teacher_gain.astype(jnp.float32) * (resid_rows.astype(jnp.float32) + attn_rows)
    inv_teacher = lax.rsqrt(lax.optimization_barrier(jnp.sum(scaled_rows * scaled_rows, axis=1, keepdims=True)) + EPS)
    return (scaled_rows * inv_teacher).astype(jnp.bfloat16)

def reference(states, lengths, norm_gain, w_gate, w_up, w_down, context, w_out, resid_stream, teacher_gain):
    attn_rows = jnp.dot(context, w_out, preferred_element_type=jnp.float32)
    teacher_rows = teacher_embed(attn_rows, resid_stream, teacher_gain)
    gram_teacher = jnp.dot(teacher_rows, teacher_rows.T, preferred_element_type=jnp.float32)
    states_wide = states.astype(jnp.float32)
    inv_rms = lax.rsqrt(lax.optimization_barrier(jnp.mean(states_wide * states_wide, axis=1, keepdims=True)) + EPS)
    normed = (states_wide * inv_rms * norm_gain.astype(jnp.float32)).astype(jnp.bfloat16)
    gate_pre = jnp.dot(normed, w_gate, preferred_element_type=jnp.float32)
    up_pre = jnp.dot(normed, w_up, preferred_element_type=jnp.float32)
    hidden = (jax.nn.silu(gate_pre) * up_pre).astype(jnp.bfloat16)
    layer_out = states_wide + jnp.dot(hidden, w_down, preferred_element_type=jnp.float32)
    positions = jnp.arange(SEQ, dtype=jnp.int32)
    valid_mask = (positions[None, :] < lengths[:, None]).astype(jnp.float32)
    counts = lengths.astype(jnp.float32)
    pooled = lax.optimization_barrier(jnp.sum(layer_out.reshape(DOCS, SEQ, SD) * valid_mask[:, :, None], axis=1)) / counts[:, None]
    inv_norm = lax.rsqrt(lax.optimization_barrier(jnp.sum(pooled * pooled, axis=1, keepdims=True)) + EPS)
    unit_rows = pooled * inv_norm
    embed_rows = unit_rows.astype(jnp.bfloat16)
    gram_student = jnp.dot(embed_rows, embed_rows.T, preferred_element_type=jnp.float32)
    gram_diff = gram_student - gram_teacher
    diff_norm = jnp.sqrt(jnp.sum(gram_diff * gram_diff) + EPS)
    teacher_norm = jnp.sqrt(jnp.sum(gram_teacher * gram_teacher))
    gram_loss = diff_norm / teacher_norm
    d_gram = LOSS_SCALE * gram_diff / (diff_norm * teacher_norm)
    d_embed = 2.0 * jnp.dot(d_gram, embed_rows.astype(jnp.float32), precision=lax.Precision.HIGHEST)
    along = lax.optimization_barrier(jnp.sum(unit_rows * d_embed, axis=1, keepdims=True))
    d_pooled = (d_embed - unit_rows * along) * inv_norm
    d_doc = (d_pooled / counts[:, None]).astype(jnp.bfloat16)
    d_token = (d_doc.astype(jnp.float32)[:, None, :] * valid_mask[:, :, None]).astype(jnp.bfloat16).reshape(TOKENS, SD)
    grad_down = jnp.dot(hidden.T, d_token, preferred_element_type=jnp.float32)
    d_hidden = jnp.dot(d_doc, w_down.T, preferred_element_type=jnp.float32)
    d_hidden_tok = (d_hidden[:, None, :] * valid_mask[:, :, None]).reshape(TOKENS, FF)
    sigmoid_gate = jax.nn.sigmoid(gate_pre)
    d_gate = (d_hidden_tok * up_pre * sigmoid_gate * (1.0 + gate_pre * (1.0 - sigmoid_gate))).astype(jnp.bfloat16)
    d_up = (d_hidden_tok * jax.nn.silu(gate_pre)).astype(jnp.bfloat16)
    grad_gate = jnp.dot(normed.T, d_gate, preferred_element_type=jnp.float32)
    grad_up = jnp.dot(normed.T, d_up, preferred_element_type=jnp.float32)
    return (gram_loss.reshape(1), grad_gate, grad_up, grad_down)
```

```python
import functools

import jax
import jax.numpy as jnp
from jax import lax
from jax.experimental import pallas as pl
from jax.experimental.pallas import tpu as pltpu
from jax.sharding import PartitionSpec as P

EPS = 1e-06
LOSS_SCALE = 4096.0
HIGHEST = lax.Precision.HIGHEST
F32 = jnp.float32
BF16 = jnp.bfloat16
LANES = 128
VMEM_LIMIT = 40 * 1024 * 1024


def params():
    return pltpu.CompilerParams(vmem_limit_bytes=VMEM_LIMIT)


def cost(flops, nbytes, trans=0):
    return pl.CostEstimate(flops=flops, bytes_accessed=nbytes, transcendentals=trans)


def vmem():
    return pl.BlockSpec(memory_space=pltpu.VMEM)


def smem():
    return pl.BlockSpec(memory_space=pltpu.SMEM)


def norm_kernel(n_chips, doc_dev, meta, lens, states, gain, normed, normed_t, state_sum, held_t):
    rows, width = states.shape
    seq = rows // doc_dev
    wide = states[...].astype(F32)
    inv = lax.rsqrt(jnp.mean(wide * wide, axis=1, keepdims=True) + EPS)
    result = (wide * inv * gain[...].astype(F32)).astype(BF16)
    slot = lax.broadcasted_iota(jnp.int32, (seq, 1), 0)
    for doc in range(doc_dev):
        part = slice(doc * seq, (doc + 1) * seq)
        valid = slot < lens[doc]
        normed[part] = jnp.where(valid, result[part].astype(F32), 0.0).astype(BF16)
        state_sum[doc : doc + 1] = jnp.sum(jnp.where(valid, wide[part], 0.0), axis=0, keepdims=True)
    held_t[...] = normed[...].T
    block = width // (2 * n_chips)
    for flip in range(n_chips):
        start = jnp.bitwise_xor(meta[0], flip) * (2 * block) + meta[1] * block
        normed_t[flip * block : (flip + 1) * block] = held_t[pl.ds(pl.multiple_of(start, block), block)]


def norm_call(n_chips, meta, lens, states, gain):
    rows, width = states.shape
    doc_dev = lens.shape[0]
    return pl.pallas_call(
        functools.partial(norm_kernel, n_chips, doc_dev),
        out_shape=(
            jax.ShapeDtypeStruct((rows, width), BF16),
            jax.ShapeDtypeStruct((width // 2, rows), BF16),
            jax.ShapeDtypeStruct((doc_dev, width), F32),
        ),
        in_specs=[smem(), smem(), vmem(), vmem()],
        out_specs=(vmem(), vmem(), vmem()),
        scratch_shapes=[pltpu.VMEM((width, rows), BF16)],
        compiler_params=params(),
        cost_estimate=cost(0, rows * width * 5),
        name="norm_rows",
    )(meta, lens, states, gain)


def forward_kernel(doc_dev, normed, w_gate, w_up, gate_factor, up_factor, hidden_sum):
    rows = normed.shape[0]
    seq = rows // doc_dev
    for doc in range(doc_dev):
        part = slice(doc * seq, (doc + 1) * seq)
        gate = jnp.dot(normed[part], w_gate[...], preferred_element_type=F32)
        up = jnp.dot(normed[part], w_up[...], preferred_element_type=F32)
        sig = jax.nn.sigmoid(gate)
        act = gate * sig
        gate_factor[part] = up * sig * (1.0 + gate * (1.0 - sig))
        up_factor[part] = act
        hidden = (act * up).astype(BF16).astype(F32)
        hidden_sum[doc : doc + 1] = jnp.sum(hidden, axis=0, keepdims=True)


def forward_call(doc_dev, at, cols, normed, w_gate, w_up):
    rows, width = normed.shape
    return pl.pallas_call(
        functools.partial(forward_kernel, doc_dev),
        out_shape=(
            jax.ShapeDtypeStruct((rows, cols), F32),
            jax.ShapeDtypeStruct((rows, cols), F32),
            jax.ShapeDtypeStruct((doc_dev, cols), F32),
        ),
        grid=(1,),
        in_specs=[
            pl.BlockSpec((rows, width), lambda i: (0, 0)),
            pl.BlockSpec((width, cols), lambda i: (0, at)),
            pl.BlockSpec((width, cols), lambda i: (0, at)),
        ],
        out_specs=(
            pl.BlockSpec((rows, cols), lambda i: (0, 0)),
            pl.BlockSpec((rows, cols), lambda i: (0, 0)),
            pl.BlockSpec((doc_dev, cols), lambda i: (0, 0)),
        ),
        compiler_params=params(),
        cost_estimate=cost(4 * rows * width * cols, 2 * rows * width + 4 * width * cols + 8 * rows * cols, rows * cols),
        name="forward_cols",
    )(normed, w_gate, w_up)


def student_kernel(hidden_width, width, rows_in, w_down, unit, inv_norm, gram):
    docs = rows_in.shape[0]
    hid = rows_in[:, :hidden_width]
    high = hid.astype(BF16)
    rest = hid - high.astype(F32)
    mid = rest.astype(BF16)
    low = (rest - mid.astype(F32)).astype(BF16)
    w = w_down[...]
    total = (
        jnp.dot(low, w, preferred_element_type=F32)
        + jnp.dot(mid, w, preferred_element_type=F32)
        + jnp.dot(high, w, preferred_element_type=F32)
    )
    count = rows_in[:, hidden_width + width : hidden_width + width + 1]
    pooled = (total + rows_in[:, hidden_width : hidden_width + width]) / count
    inv = lax.rsqrt(jnp.sum(pooled * pooled, axis=1, keepdims=True) + EPS)
    rows = pooled * inv
    unit[...] = rows
    inv_norm[...] = jnp.broadcast_to(inv, (docs, LANES))
    embed = rows.astype(BF16)
    gram[...] = lax.dot_general(embed, embed, (((1,), (1,)), ((), ())), preferred_element_type=F32)


def student_call(rows_in, w_down):
    hidden_width, width = w_down.shape
    docs = rows_in.shape[0]
    return pl.pallas_call(
        functools.partial(student_kernel, hidden_width, width),
        out_shape=(
            jax.ShapeDtypeStruct((docs, width), F32),
            jax.ShapeDtypeStruct((docs, LANES), F32),
            jax.ShapeDtypeStruct((docs, docs), F32),
        ),
        in_specs=[vmem(), vmem()],
        out_specs=(vmem(), vmem(), vmem()),
        compiler_params=params(),
        cost_estimate=cost(6 * docs * width * hidden_width, 2 * width * hidden_width),
        name="student_rows",
    )(rows_in, w_down)


def loss_kernel(doc_dev, meta, products, unit, inv_norm, gram_student, counts, w_down, loss, d_doc, d_hidden):
    docs = unit.shape[0]
    prod = products[...]
    at_row = lax.broadcasted_iota(jnp.int32, (docs, docs), 0)
    at_col = lax.broadcasted_iota(jnp.int32, (docs, docs), 1)
    me = meta[0] * 2 + meta[1]
    owner = jnp.bitwise_xor(at_row // doc_dev, me)
    pick = (at_col == owner * doc_dev + at_row % doc_dev).astype(F32)
    prod = jnp.dot(pick, prod, precision=HIGHEST, preferred_element_type=F32)
    prod = lax.dot_general(prod, pick, (((1,), (1,)), ((), ())), precision=HIGHEST, preferred_element_type=F32)
    own = jnp.where(at_row == at_col, prod, 0.0)
    gram_teacher = (
        prod
        * lax.rsqrt(jnp.sum(own, axis=1, keepdims=True) + EPS)
        * lax.rsqrt(jnp.sum(own, axis=0, keepdims=True) + EPS)
    )
    gram_diff = gram_student[...] - gram_teacher
    diff_norm = jnp.sqrt(jnp.sum(gram_diff * gram_diff, keepdims=True) + EPS)
    teacher_norm = jnp.sqrt(jnp.sum(gram_teacher * gram_teacher, keepdims=True))
    loss[...] = jnp.broadcast_to(diff_norm / teacher_norm, loss.shape)
    d_gram = LOSS_SCALE * gram_diff / (diff_norm * teacher_norm)
    rows = unit[...]
    embed = rows.astype(BF16).astype(F32)
    d_embed = 2.0 * jnp.dot(d_gram, embed, precision=HIGHEST, preferred_element_type=F32)
    along = jnp.sum(rows * d_embed, axis=1, keepdims=True)
    d_pooled = (d_embed - rows * along) * inv_norm[:, 0:1]
    result = (d_pooled / counts[:, 0:1]).astype(BF16)
    d_doc[...] = result
    near = d_hidden.shape[0]
    d_hidden[...] = lax.dot_general(
        result[:near], w_down[...], (((1,), (1,)), ((), ())), preferred_element_type=F32
    )


def loss_call(doc_dev, meta, products, unit, inv_norm, gram_student, counts, w_down):
    docs, width = unit.shape
    hidden_width = w_down.shape[0]
    near = min(16, docs)
    return pl.pallas_call(
        functools.partial(loss_kernel, doc_dev),
        out_shape=(
            jax.ShapeDtypeStruct((1, LANES), F32),
            jax.ShapeDtypeStruct((docs, width), BF16),
            jax.ShapeDtypeStruct((near, hidden_width), F32),
        ),
        in_specs=[smem()] + [vmem()] * 6,
        out_specs=(vmem(), vmem(), vmem()),
        compiler_params=params(),
        cost_estimate=cost(2 * near * width * hidden_width, 2 * width * hidden_width),
        name="loss_rows",
    )(meta, products, unit, inv_norm, gram_student, counts, w_down)


def backward_kernel(doc_dev, sent_flips, kept_flips, d_hidden, n_own, n_pair, g_own, g_pair, u_own, u_pair, sent, kept):
    cols = g_own.shape[1]
    block = sent.shape[1]
    seq = g_own.shape[0] // doc_dev
    for part, factors in enumerate(((g_own, g_pair), (u_own, u_pair))):
        total = None
        for side, (rows_t, factor) in enumerate(zip((n_own, n_pair), factors)):
            scaled = []
            for doc in range(doc_dev):
                at = side * doc_dev + doc
                scaled.append((factor[doc * seq : (doc + 1) * seq] * d_hidden[at : at + 1]).astype(BF16))
            term = jnp.dot(rows_t[...], jnp.concatenate(scaled, axis=0), preferred_element_type=F32)
            total = term if total is None else total + term
        place = slice(part * cols, (part + 1) * cols)
        for at, flip in enumerate(sent_flips):
            sent[at, :, place] = total[flip * block : (flip + 1) * block].astype(BF16)
        for at, flip in enumerate(kept_flips):
            kept[at, :, place] = total[flip * block : (flip + 1) * block]


def backward_call(doc_dev, at, sent_flips, kept_flips, d_hidden, n_own, n_pair, g_own, g_pair, u_own, u_pair):
    half, rows = n_own.shape
    cols = g_own.shape[1]
    count = len(sent_flips)
    block = half // (2 * count)
    whole = lambda shape: pl.BlockSpec(shape, lambda i: (0,) * len(shape))
    return pl.pallas_call(
        functools.partial(backward_kernel, doc_dev, sent_flips, kept_flips),
        out_shape=(
            jax.ShapeDtypeStruct((count, block, 2 * cols), BF16),
            jax.ShapeDtypeStruct((count, block, 2 * cols), F32),
        ),
        grid=(1,),
        in_specs=[pl.BlockSpec((d_hidden.shape[0], cols), lambda i: (0, at))]
        + [whole((half, rows))] * 2
        + [whole((rows, cols))] * 4,
        out_specs=(whole((count, block, 2 * cols)), whole((count, block, 2 * cols))),
        compiler_params=params(),
        cost_estimate=cost(8 * half * rows * cols, 16 * rows * cols + 4 * half * rows + 6 * half * cols),
        name="backward_cols",
    )(d_hidden, n_own, n_pair, g_own, g_pair, u_own, u_pair)


def per_device(
    n_dev, states, lengths, norm_gain, w_gate, w_up, w_down, context, w_out, resid_stream, teacher_gain
):
    n_chips = n_dev // 2
    doc_dev = lengths.shape[0]
    width, hidden_width = w_gate.shape
    docs = doc_dev * n_dev
    me = lax.axis_index("dp")
    meta = jnp.stack([me // 2, me % 2]).astype(jnp.int32)
    bits = [1 << k for k in range(n_dev.bit_length() - 1)]

    def swap(x, flip):
        return lax.ppermute(x, "dp", [(i, i ^ flip) for i in range(n_dev)])

    attn = jnp.dot(context, w_out, preferred_element_type=F32)
    states_pair = swap(states, 1)
    lengths_pair = swap(lengths, 1)
    first = jnp.zeros((), jnp.int32)
    for bit in bits:
        half = attn.shape[1] // 2
        upper = (me // bit) % 2
        other = swap(lax.dynamic_slice_in_dim(attn, (1 - upper) * half, half, 1), bit)
        attn = lax.dynamic_slice_in_dim(attn, upper * half, half, 1) + other
        first = first + upper * half
    part = attn.shape[1]
    resid_part = lax.dynamic_slice_in_dim(resid_stream, first, part, 1).astype(F32)
    gain_part = lax.dynamic_slice_in_dim(teacher_gain, first, part, 0).astype(F32)
    rows = gain_part * (resid_part + attn)
    products = lax.dot_general(
        rows, rows, (((1,), (1,)), ((), ())), precision=HIGHEST, preferred_element_type=F32
    )
    for bit in bits:
        products = products + swap(products, bit)

    n_blocks = 3
    cols = hidden_width // n_blocks
    gain = norm_gain.reshape(1, width)
    normed, n_own, state_sum = norm_call(n_chips, meta, lengths, states, gain)
    own = [forward_call(doc_dev, at, cols, normed, w_gate, w_up) for at in range(n_blocks)]
    counts = jnp.broadcast_to(lengths.astype(F32)[:, None], (doc_dev, LANES))
    gathered = jnp.concatenate([o[2] for o in own] + [state_sum, counts], axis=1)
    normed_pair, n_pair, _ = norm_call(n_chips, meta, lengths_pair, states_pair, gain)
    pair = [forward_call(doc_dev, at, cols, normed_pair, w_gate, w_up) for at in range(n_blocks)]
    for bit in bits:
        gathered = jnp.concatenate([gathered, swap(gathered, bit)], axis=0)
    unit, inv_norm, gram_student = student_call(gathered, w_down)
    loss, d_doc, d_hidden = loss_call(
        doc_dev, meta, products, unit, inv_norm, gram_student, gathered[:, hidden_width + width :], w_down
    )

    chip_bits = [1 << k for k in range(n_chips.bit_length() - 1)]
    results = []
    for at in range(n_blocks):
        order = chip_bits
        flips = list(range(n_chips))
        step = order[0]
        later = order[1:]
        key = lambda f: tuple(-((f // b) % 2) for b in later)
        sent_flips = sorted([f for f in flips if f & step], key=key)
        kept_flips = [f ^ step for f in sent_flips]
        sent, kept = backward_call(
            doc_dev, at, sent_flips, kept_flips, d_hidden, n_own, n_pair, own[at][0], pair[at][0], own[at][1], pair[at][1]
        )
        for stage, step in enumerate(order):
            got = swap(sent, 2 * step)
            half = got.shape[0] // 2
            if half:
                sent = (kept[:half] + got[:half].astype(F32)).astype(BF16)
                kept = kept[half:] + got[half:].astype(F32)
            else:
                kept = kept + got.astype(F32)
        results.append(kept[0])
    grad_gate = jnp.concatenate([r[:, :cols] for r in results], axis=1)
    grad_up = jnp.concatenate([r[:, cols:] for r in results], axis=1)

    slot = hidden_width // n_dev
    hidden_part = lax.dynamic_slice_in_dim(gathered, me * slot, slot, 1)
    grad_down = lax.dot_general(
        hidden_part, d_doc.astype(F32), (((0,), (0,)), ((), ())), precision=HIGHEST, preferred_element_type=F32
    )
    return (loss[0, :1], grad_gate, grad_up, grad_down)


def solution(mesh):
    in_specs = (
        P(("groups", "dp"), None),
        P(("groups", "dp")),
        P(),
        P(),
        P(),
        P(),
        P("groups", "dp"),
        P("dp", None),
        P("groups", None),
        P(),
    )
    out_specs = (
        P("groups"),
        P(("groups", "dp"), None),
        P(("groups", "dp"), None),
        P(("groups", "dp"), None),
    )
    return jax.shard_map(
        functools.partial(per_device, mesh.shape["dp"]),
        mesh=mesh,
        in_specs=in_specs,
        out_specs=out_specs,
        check_vma=False,
    )
```

```python
import functools

import jax
import jax.numpy as jnp
from jax import lax
from jax.experimental import pallas as pl
from jax.experimental.pallas import tpu as pltpu
from jax.sharding import PartitionSpec as P

EPS = 1e-06
LOSS_SCALE = 4096.0
HIGHEST = lax.Precision.HIGHEST
F32 = jnp.float32
BF16 = jnp.bfloat16
LANES = 128


def params(mib=16):
    return pltpu.CompilerParams(vmem_limit_bytes=mib * 1024 * 1024)


def cost(flops, nbytes, trans=0):
    return pl.CostEstimate(flops=flops, bytes_accessed=nbytes, transcendentals=trans)


def vmem():
    return pl.BlockSpec(memory_space=pltpu.VMEM)


def smem():
    return pl.BlockSpec(memory_space=pltpu.SMEM)


def norm_kernel(row_flips, doc_dev, meta, states, gain, normed, normed_t, state_sum, held_t):
    rows, width = states.shape
    seq = rows // doc_dev
    wide = states[...].astype(F32)
    inv = lax.rsqrt(jnp.mean(wide * wide, axis=1, keepdims=True) + EPS)
    normed[...] = (wide * inv * gain[...].astype(F32)).astype(BF16)
    for doc in range(doc_dev if state_sum is not None else 0):
        state_sum[doc : doc + 1] = jnp.sum(wide[doc * seq : (doc + 1) * seq], axis=0, keepdims=True)
    held_t[...] = normed[...].T
    block = normed_t.shape[0] // len(row_flips)
    for at, flip in enumerate(row_flips):
        start = jnp.bitwise_xor(meta[0], flip) * block
        normed_t[at * block : (at + 1) * block] = held_t[pl.ds(pl.multiple_of(start, block), block)]


def other_norm_kernel(row_flips, doc_dev, meta, states, gain, normed, normed_t, held_t):
    norm_kernel(row_flips, doc_dev, meta, states, gain, normed, normed_t, None, held_t)


def norm_call(n_dev, row_flips, doc_dev, meta, states, gain):
    rows, width = states.shape
    return pl.pallas_call(
        functools.partial(other_norm_kernel, row_flips, doc_dev),
        out_shape=(
            jax.ShapeDtypeStruct((rows, width), BF16),
            jax.ShapeDtypeStruct((width // n_dev * len(row_flips), rows), BF16),
        ),
        in_specs=[smem(), vmem(), vmem()],
        out_specs=(vmem(), vmem()),
        scratch_shapes=[pltpu.VMEM((width, rows), BF16)],
        compiler_params=params(),
        cost_estimate=cost(0, rows * width * 5),
        name="norm_rows",
    )(meta, states, gain)


def hbm():
    return pl.BlockSpec(memory_space=pltpu.MemorySpace.HBM)


def factor_rows(doc_dev, normed, w_gate, w_up, gate_factor, up_factor, hidden_sum):
    rows = normed.shape[0]
    seq = rows // doc_dev
    for doc in range(doc_dev):
        part = slice(doc * seq, (doc + 1) * seq)
        gate = jnp.dot(normed[part], w_gate[...], preferred_element_type=F32)
        up = jnp.dot(normed[part], w_up[...], preferred_element_type=F32)
        sig = jax.nn.sigmoid(gate)
        act = gate * sig
        gate_factor[part] = (up * sig * (1.0 + gate * (1.0 - sig))).astype(BF16)
        up_factor[part] = act.astype(BF16)
        if hidden_sum is not None:
            hidden = (act * up).astype(BF16).astype(F32)
            hidden_sum[doc : doc + 1] = jnp.sum(hidden, axis=0, keepdims=True)


def own_kernel(row_flips, doc_dev, n_blocks, meta, lens, states, gain, w_gate, w_up, *refs):
    normed_t = refs[0]
    factors = refs[1 : 1 + 2 * n_blocks]
    sums = refs[1 + 2 * n_blocks]
    normed, held_t, held_w, sems = refs[2 + 2 * n_blocks :]
    width = states.shape[1]
    cols = w_gate.shape[1] // n_blocks
    hidden_width = w_gate.shape[1]
    copies = []
    for at in range(n_blocks):
        for kind, w in enumerate((w_gate, w_up)):
            copy = pltpu.make_async_copy(
                w.at[:, at * cols : (at + 1) * cols], held_w.at[kind, at], sems.at[kind, at]
            )
            copy.start()
            copies.append(copy)
    norm_kernel(
        row_flips, doc_dev, meta, states, gain, normed, normed_t, sums.at[:, hidden_width : hidden_width + width], held_t
    )
    for doc in range(doc_dev):
        sums[doc : doc + 1, hidden_width + width :] = jnp.full((1, LANES), lens[doc], jnp.int32).astype(F32)
    for at in range(n_blocks):
        copies[2 * at].wait()
        copies[2 * at + 1].wait()
        factor_rows(
            doc_dev, normed, held_w.at[0, at], held_w.at[1, at], factors[2 * at], factors[2 * at + 1],
            sums.at[:, at * cols : (at + 1) * cols],
        )


def own_call(n_dev, row_flips, n_blocks, meta, lens, states, gain, w_gate, w_up):
    rows, width = states.shape
    hidden_width = w_gate.shape[1]
    cols = hidden_width // n_blocks
    doc_dev = lens.shape[0]
    return pl.pallas_call(
        functools.partial(own_kernel, row_flips, doc_dev, n_blocks),
        out_shape=(jax.ShapeDtypeStruct((width // n_dev * len(row_flips), rows), BF16),)
        + (jax.ShapeDtypeStruct((rows, cols), BF16),) * (2 * n_blocks)
        + (jax.ShapeDtypeStruct((doc_dev, hidden_width + width + LANES), F32),),
        in_specs=[smem(), smem(), vmem(), vmem(), hbm(), hbm()],
        out_specs=(vmem(),) * (2 + 2 * n_blocks),
        scratch_shapes=[
            pltpu.VMEM((rows, width), BF16),
            pltpu.VMEM((width, rows), BF16),
            pltpu.VMEM((2, n_blocks, width, cols), BF16),
            pltpu.SemaphoreType.DMA((2, n_blocks)),
        ],
        compiler_params=params(24),
        cost_estimate=cost(4 * rows * width * hidden_width, 4 * width * hidden_width, rows * hidden_width),
        name="own_rows",
    )(meta, lens, states, gain, w_gate, w_up)


def forward_kernel(doc_dev, normed, w_gate, w_up, gate_factor, up_factor):
    factor_rows(doc_dev, normed, w_gate, w_up, gate_factor, up_factor, None)


def forward_call(doc_dev, at, cols, normed, w_gate, w_up):
    rows, width = normed.shape
    return pl.pallas_call(
        functools.partial(forward_kernel, doc_dev),
        out_shape=(
            jax.ShapeDtypeStruct((rows, cols), BF16),
            jax.ShapeDtypeStruct((rows, cols), BF16),
        ),
        grid=(1,),
        in_specs=[
            pl.BlockSpec((rows, width), lambda i: (0, 0)),
            pl.BlockSpec((width, cols), lambda i: (0, at)),
            pl.BlockSpec((width, cols), lambda i: (0, at)),
        ],
        out_specs=(
            pl.BlockSpec((rows, cols), lambda i: (0, 0)),
            pl.BlockSpec((rows, cols), lambda i: (0, 0)),
        ),
        compiler_params=params(),
        cost_estimate=cost(4 * rows * width * cols, 2 * rows * width + 4 * width * cols + 8 * rows * cols, rows * cols),
        name="forward_cols",
    )(normed, w_gate, w_up)


def student_kernel(pieces, rows_in, w_down, unit, inv_norm, gram, held_w, sems):
    hidden_width, width = held_w.shape
    docs = rows_in.shape[0]
    step = hidden_width // pieces
    copies = []
    for at in range(pieces):
        part = pl.ds(at * step, step)
        copy = pltpu.make_async_copy(w_down.at[part], held_w.at[part], sems.at[at])
        copy.start()
        copies.append(copy)
    hid = rows_in[:, :hidden_width]
    high = hid.astype(BF16)
    rest = hid - high.astype(F32)
    mid = rest.astype(BF16)
    low = (rest - mid.astype(F32)).astype(BF16)
    split = jnp.concatenate([low, mid, high], axis=0)
    total = None
    for at in range(pieces):
        copies[at].wait()
        part = slice(at * step, (at + 1) * step)
        term = jnp.dot(split[:, part], held_w[part], preferred_element_type=F32)
        total = term if total is None else total + term
    total = total[:docs] + total[docs : 2 * docs] + total[2 * docs :]
    count = rows_in[:, hidden_width + width : hidden_width + width + 1]
    pooled = (total + rows_in[:, hidden_width : hidden_width + width]) / count
    inv = lax.rsqrt(jnp.sum(pooled * pooled, axis=1, keepdims=True) + EPS)
    rows = pooled * inv
    unit[...] = rows
    inv_norm[...] = jnp.broadcast_to(inv, (docs, LANES))
    embed = rows.astype(BF16)
    gram[...] = lax.dot_general(embed, embed, (((1,), (1,)), ((), ())), preferred_element_type=F32)


def student_call(rows_in, w_down):
    hidden_width, width = w_down.shape
    docs = rows_in.shape[0]
    pieces = 6
    return pl.pallas_call(
        functools.partial(student_kernel, pieces),
        out_shape=(
            jax.ShapeDtypeStruct((docs, width), F32),
            jax.ShapeDtypeStruct((docs, LANES), F32),
            jax.ShapeDtypeStruct((docs, docs), F32),
        ),
        in_specs=[vmem(), hbm()],
        out_specs=(vmem(), vmem(), vmem()),
        scratch_shapes=[pltpu.VMEM((hidden_width, width), BF16), pltpu.SemaphoreType.DMA((pieces,))],
        compiler_params=params(),
        cost_estimate=cost(6 * docs * width * hidden_width, 2 * width * hidden_width),
        name="student_rows",
    )(rows_in, w_down)


def loss_kernel(doc_dev, gather_bits, near_at, meta, products, unit, inv_norm, gram_student, rows_in, w_down, loss, d_doc, d_hidden, held_w, sems):
    docs = unit.shape[0]
    pieces = sems.shape[0]
    step = held_w.shape[0] // pieces
    copies = []
    for at in range(pieces):
        part = pl.ds(at * step, step)
        copy = pltpu.make_async_copy(w_down.at[part], held_w.at[part], sems.at[at])
        copy.start()
        copies.append(copy)
    prod = products[...]
    at_row = lax.broadcasted_iota(jnp.int32, (docs, docs), 0)
    at_col = lax.broadcasted_iota(jnp.int32, (docs, docs), 1)
    owner = meta[0]
    for place, bit in enumerate(gather_bits):
        owner = jnp.bitwise_xor(owner, jnp.bitwise_and((at_row // doc_dev) >> place, 1) * bit)
    pick = (at_col == owner * doc_dev + at_row % doc_dev).astype(F32)
    prod = jnp.dot(pick, prod, precision=HIGHEST, preferred_element_type=F32)
    prod = lax.dot_general(prod, pick, (((1,), (1,)), ((), ())), precision=HIGHEST, preferred_element_type=F32)
    own = jnp.where(at_row == at_col, prod, 0.0)
    gram_teacher = (
        prod
        * lax.rsqrt(jnp.sum(own, axis=1, keepdims=True) + EPS)
        * lax.rsqrt(jnp.sum(own, axis=0, keepdims=True) + EPS)
    )
    gram_diff = gram_student[...] - gram_teacher
    diff_norm = jnp.sqrt(jnp.sum(gram_diff * gram_diff, keepdims=True) + EPS)
    teacher_norm = jnp.sqrt(jnp.sum(gram_teacher * gram_teacher, keepdims=True))
    loss[...] = jnp.broadcast_to(diff_norm / teacher_norm, loss.shape)
    d_gram = LOSS_SCALE * gram_diff / (diff_norm * teacher_norm)
    rows = unit[...]
    embed = rows.astype(BF16).astype(F32)
    d_embed = 2.0 * jnp.dot(d_gram, embed, precision=HIGHEST, preferred_element_type=F32)
    along = jnp.sum(rows * d_embed, axis=1, keepdims=True)
    d_pooled = (d_embed - rows * along) * inv_norm[:, 0:1]
    count_at = held_w.shape[0] + held_w.shape[1]
    result = d_pooled / rows_in[:, count_at : count_at + 1]
    d_doc[...] = result.astype(BF16)
    near = jnp.concatenate([result[at : at + doc_dev] for at in near_at], axis=0).astype(BF16)
    for at in range(pieces):
        copies[at].wait()
        part = slice(at * step, (at + 1) * step)
        d_hidden[:, part] = lax.dot_general(near, held_w[part], (((1,), (1,)), ((), ())), preferred_element_type=F32)


def loss_call(doc_dev, gather_bits, near_at, meta, products, unit, inv_norm, gram_student, rows_in, w_down):
    docs, width = unit.shape
    hidden_width = w_down.shape[0]
    near = doc_dev * len(near_at)
    return pl.pallas_call(
        functools.partial(loss_kernel, doc_dev, gather_bits, near_at),
        out_shape=(
            jax.ShapeDtypeStruct((1, LANES), F32),
            jax.ShapeDtypeStruct((docs, width), BF16),
            jax.ShapeDtypeStruct((near, hidden_width), F32),
        ),
        in_specs=[smem()] + [vmem()] * 5 + [hbm()],
        out_specs=(vmem(), vmem(), vmem()),
        scratch_shapes=[pltpu.VMEM((hidden_width, width), BF16), pltpu.SemaphoreType.DMA((6,))],
        compiler_params=params(),
        cost_estimate=cost(2 * near * width * hidden_width, 2 * width * hidden_width),
        name="loss_rows",
    )(meta, products, unit, inv_norm, gram_student, rows_in, w_down)


def backward_kernel(doc_dev, shares, row_flips, sent_flips, kept_flips, d_hidden, *refs):
    rows_t, gates, ups = refs[:shares], refs[shares : 2 * shares], refs[2 * shares : 3 * shares]
    sent, kept = refs[3 * shares :]
    cols = gates[0].shape[1]
    block = sent.shape[1]
    seq = gates[0].shape[0] // doc_dev
    for part, factors in enumerate((gates, ups)):
        total = None
        for side, factor in enumerate(factors):
            scaled = []
            for doc in range(doc_dev):
                at = side * doc_dev + doc
                scaled.append((factor[doc * seq : (doc + 1) * seq].astype(F32) * d_hidden[at : at + 1]).astype(BF16))
            term = jnp.dot(rows_t[side][...], jnp.concatenate(scaled, axis=0), preferred_element_type=F32)
            total = term if total is None else total + term
        place = slice(part * cols, (part + 1) * cols)
        for out, flips in ((sent, sent_flips), (kept, kept_flips)):
            for at, flip in enumerate(flips):
                start = row_flips.index(flip) * block
                out[at, :, place] = total[start : start + block].astype(out.dtype)


def backward_call(doc_dev, at, row_flips, sent_flips, kept_flips, d_hidden, rows_t, gates, ups):
    height, rows = rows_t[0].shape
    cols = gates[0].shape[1]
    shares = len(gates)
    count = len(sent_flips)
    block = height // len(row_flips)
    whole = lambda shape: pl.BlockSpec(shape, lambda i: (0,) * len(shape))
    return pl.pallas_call(
        functools.partial(backward_kernel, doc_dev, shares, row_flips, sent_flips, kept_flips),
        out_shape=(
            jax.ShapeDtypeStruct((count, block, 2 * cols), BF16),
            jax.ShapeDtypeStruct((count, block, 2 * cols), F32),
        ),
        grid=(1,),
        in_specs=[pl.BlockSpec((d_hidden.shape[0], cols), lambda i: (0, at))]
        + [whole((height, rows))] * shares
        + [whole((rows, cols))] * (2 * shares),
        out_specs=(whole((count, block, 2 * cols)), whole((count, block, 2 * cols))),
        compiler_params=params(),
        cost_estimate=cost(4 * shares * height * rows * cols, 4 * shares * rows * cols + 2 * shares * height * rows + 6 * height * cols),
        name="backward_cols",
    )(d_hidden, *rows_t, *gates, *ups)


def tie(x, *others):
    return lax.optimization_barrier((x,) + others)[0]


def per_device(
    n_dev, states, lengths, norm_gain, w_gate, w_up, w_down, context, w_out, resid_stream, teacher_gain
):
    doc_dev = lengths.shape[0]
    width, hidden_width = w_gate.shape
    seq = states.shape[0] // doc_dev
    me = lax.axis_index("dp")
    meta = me.astype(jnp.int32).reshape(1)
    bits = [1 << k for k in range(n_dev.bit_length() - 1)]
    near = 2
    share = (0, 1, near, near ^ 1)
    sum_bits = [b for b in bits if b not in share]
    gather_bits = bits[::-1]

    def span(some):
        flips = [0]
        for bit in some:
            flips = flips + [f ^ bit for f in flips]
        return flips

    row_flips = span(sum_bits)
    gather_flips = span(gather_bits)
    near_at = [gather_flips.index(f) * doc_dev for f in share]

    def swap(x, flip):
        return lax.ppermute(x, "dp", [(i, i ^ flip) for i in range(n_dev)])

    n_blocks = 3
    cols = hidden_width // n_blocks
    gain = norm_gain.reshape(1, width)

    teacher_bits = [b for b in bits if b != near] + [near]

    attn = jnp.dot(context, w_out, preferred_element_type=F32)
    slot_at = lax.broadcasted_iota(jnp.int32, (doc_dev, seq, 1), 1)
    valid = slot_at < lengths[:, None, None]
    masked = jnp.where(valid, states.reshape(doc_dev, seq, width), jnp.zeros((), BF16)).reshape(states.shape)
    states_of = {0: masked}
    states_of[near] = swap(masked, near)
    states_of[1] = swap(masked, 1)
    normed_of, rows_t, factors = {}, {}, {}

    def norm(flip, *after):
        normed_of[flip], rows_t[flip] = norm_call(
            n_dev, row_flips, doc_dev, meta, tie(states_of[flip], *after), gain
        )
        return rows_t[flip]

    def forward(flip, at, *after):
        factors[flip, at] = forward_call(doc_dev, at, cols, tie(normed_of[flip], *after), w_gate, w_up)
        return factors[flip, at][0]

    state = {}

    def gather_step(after):
        if state["bits"]:
            mine = tie(state["rows"], after)
            state["rows"] = jnp.concatenate([mine, swap(mine, state["bits"].pop(0))], axis=0)

    def beside(step, after):
        if step == 0:
            return ()
        if step == 1:
            outs = own_call(n_dev, row_flips, n_blocks, meta, lengths, tie(masked, after), gain, w_gate, w_up)
            rows_t[0] = outs[0]
            for at in range(n_blocks):
                factors[0, at] = outs[1 + 2 * at : 3 + 2 * at]
            state["rows"] = outs[-1]
            state["bits"] = list(gather_bits)
            return (state["rows"],)
        gather_step(after)
        if step == 2:
            return (norm(1, after),)
        if step == 3:
            return (forward(1, 0, after),)
        if step == 4:
            states_of[near ^ 1] = swap(tie(states_of[near], after), 1)
            return (norm(near, after),)
        if step == 5:
            return (forward(near, 0, after), norm(near ^ 1, after))
        if step == 6:
            return (forward(near ^ 1, 0, after),)
        return ()

    first = jnp.zeros((), jnp.int32)
    before = ()
    for step, bit in enumerate(teacher_bits):
        if step + 1 < len(bits):
            half = attn.shape[1] // 2
            upper = (me // bit) % 2
            send = tie(lax.dynamic_slice_in_dim(attn, (1 - upper) * half, half, 1), *before)
            attn = lax.dynamic_slice_in_dim(attn, upper * half, half, 1)
            first = first + upper * half
        else:
            send = attn = tie(attn, *before)
        before = beside(step, send)
        attn = attn + swap(send, bit)
    part = attn.shape[1]
    resid_part = lax.dynamic_slice_in_dim(resid_stream, first, part, 1).astype(F32)
    gain_part = lax.dynamic_slice_in_dim(teacher_gain, first, part, 0).astype(F32)
    rows = gain_part * (resid_part + attn)
    products = lax.dot_general(
        rows, rows, (((1,), (1,)), ((), ())), precision=HIGHEST, preferred_element_type=F32
    )
    for step, bit in enumerate(reversed(teacher_bits[:-1])):
        products = tie(products, *before)
        before = beside(len(bits) + step, products)
        products = products + swap(products, bit)
    while state["bits"]:
        gather_step(products)
    gathered = state["rows"]
    unit, inv_norm, gram_student = student_call(gathered, w_down)
    loss, d_doc, d_hidden = loss_call(
        doc_dev, gather_bits, near_at, meta, tie(products, *before), unit, inv_norm, gram_student, gathered, w_down
    )

    results = []
    order = sum_bits
    key = lambda f: tuple(-((f & b) != 0) for b in order[1:])
    sent_flips = sorted([f for f in row_flips if f & order[0]], key=key)
    kept_flips = [f ^ order[0] for f in sent_flips]
    sent = d_hidden
    for at in range(n_blocks):
        for flip in share:
            if (flip, at) not in factors:
                forward(flip, at, sent)
        sent, kept = backward_call(
            doc_dev, at, row_flips, sent_flips, kept_flips, d_hidden,
            [rows_t[f] for f in share], [factors[f, at][0] for f in share], [factors[f, at][1] for f in share],
        )
        part = sent
        for step in order:
            got = swap(part, step)
            half = got.shape[0] // 2
            if half:
                part = (kept[:half] + got[:half].astype(F32)).astype(BF16)
                kept = kept[half:] + got[half:].astype(F32)
            else:
                kept = kept + got.astype(F32)
        results.append(kept[0])
    grad_gate = jnp.concatenate([r[:, :cols] for r in results], axis=1)
    grad_up = jnp.concatenate([r[:, cols:] for r in results], axis=1)

    slot = hidden_width // n_dev
    hidden_part = lax.dynamic_slice_in_dim(gathered, me * slot, slot, 1)
    grad_down = lax.dot_general(
        hidden_part, d_doc.astype(F32), (((0,), (0,)), ((), ())), precision=HIGHEST, preferred_element_type=F32
    )
    return (loss[0, :1], grad_gate, grad_up, grad_down)


def solution(mesh):
    in_specs = (
        P(("groups", "dp"), None),
        P(("groups", "dp")),
        P(),
        P(),
        P(),
        P(),
        P("groups", "dp"),
        P("dp", None),
        P("groups", None),
        P(),
    )
    out_specs = (
        P("groups"),
        P(("groups", "dp"), None),
        P(("groups", "dp"), None),
        P(("groups", "dp"), None),
    )
    return jax.shard_map(
        functools.partial(per_device, mesh.shape["dp"]),
        mesh=mesh,
        in_specs=in_specs,
        out_specs=out_specs,
        check_vma=False,
    )
```

```python
import functools

import jax
import jax.numpy as jnp
from jax import lax
from jax.experimental import pallas as pl
from jax.experimental.pallas import tpu as pltpu
from jax.sharding import PartitionSpec as P

EPS = 1e-06
LOSS_SCALE = 4096.0
HIGHEST = lax.Precision.HIGHEST
F32 = jnp.float32
BF16 = jnp.bfloat16
LANES = 128
PIECES = 6


def params(mib=16):
    return pltpu.CompilerParams(vmem_limit_bytes=mib * 1024 * 1024)


def cost():
    return pl.CostEstimate(flops=1024, bytes_accessed=1024, transcendentals=0)


def vmem():
    return pl.BlockSpec(memory_space=pltpu.VMEM)


def smem():
    return pl.BlockSpec(memory_space=pltpu.SMEM)


def hbm():
    return pl.BlockSpec(memory_space=pltpu.HBM)


def near_out(shape, dtype):
    return pltpu.VMEM(shape, dtype)


def near_in(x):
    return pltpu.with_memory_space_constraint(x, pltpu.VMEM)


def far_in(x):
    return pltpu.with_memory_space_constraint(x, pltpu.HBM)


def start_pieces(source, target, sems):
    pieces = sems.shape[0]
    step = target.shape[0] // pieces
    copies = []
    for at in range(pieces):
        part = pl.ds(at * step, step)
        copies.append(pltpu.make_async_copy(source.at[part], target.at[part], sems.at[at]))
        copies[-1].start()
    return copies


def rows_product(left, right, precision=None):
    return lax.dot_general(
        left, right, (((1,), (1,)), ((), ())), precision=precision, preferred_element_type=F32
    )


def arrange_kernel(pieces, piece, attn, sent, kept):
    step = attn.shape[1] // pieces
    for out, first in ((sent, pieces // 2), (kept, 0)):
        for at in range(pieces // 2):
            start = jnp.bitwise_xor(piece[0], first + at) * step
            out[:, at * step : (at + 1) * step] = attn[:, pl.ds(pl.multiple_of(start, step), step)]


def arrange_call(pieces, piece, attn):
    docs, features = attn.shape
    return pl.pallas_call(
        functools.partial(arrange_kernel, pieces),
        out_shape=(jax.ShapeDtypeStruct((docs, features // 2), F32),) * 2,
        in_specs=[smem(), vmem()],
        out_specs=(vmem(), vmem()),
        compiler_params=params(),
        cost_estimate=cost(),
        name="arrange_rows",
    )(piece, attn)


def fold_kernel(kept, got, send, keep):
    half = keep.shape[1]
    send[...] = kept[:, half:] + got[:, half:]
    keep[...] = kept[:, :half] + got[:, :half]


def fold_call(kept, got):
    docs, width = kept.shape
    return pl.pallas_call(
        fold_kernel,
        out_shape=(jax.ShapeDtypeStruct((docs, width // 2), F32),) * 2,
        in_specs=[vmem(), vmem()],
        out_specs=(vmem(), vmem()),
        compiler_params=params(),
        cost_estimate=cost(),
        name="fold_rows",
    )(kept, got)


def fold_last_kernel(kept, got, keep):
    keep[...] = kept[...] + got[...]


def fold_last_call(kept, got):
    return pl.pallas_call(
        fold_last_kernel,
        out_shape=jax.ShapeDtypeStruct(kept.shape, F32),
        in_specs=[vmem(), vmem()],
        out_specs=vmem(),
        compiler_params=params(),
        cost_estimate=cost(),
        name="fold_last",
    )(kept, got)


def gram_kernel(piece, attn, got, resid, gain, products):
    step = attn.shape[1]
    cols = pl.ds(pl.multiple_of(piece[0] * step, step), step)
    rows = gain[:, cols].astype(F32) * (resid[:, cols].astype(F32) + (attn[...] + got[...]))
    products[...] = rows_product(rows, rows, HIGHEST)


def gram_call(piece, attn, got, resid, gain):
    docs = attn.shape[0]
    return pl.pallas_call(
        gram_kernel,
        out_shape=jax.ShapeDtypeStruct((docs, docs), F32),
        in_specs=[smem()] + [vmem()] * 4,
        out_specs=vmem(),
        compiler_params=params(),
        cost_estimate=cost(),
        name="gram_terms",
    )(piece, attn, got, resid, gain)


def norm_rows(row_flips, me, lens, states, gain, normed, normed_t, held_t, sums=None):
    docs = lens.shape[0]
    seq = normed.shape[0] // docs
    first = 0
    for piece in states:
        for start in range(0, piece.shape[0], LANES):
            rows = slice(first + start, first + start + LANES)
            doc, at = divmod(rows.start, seq)
            slot = lax.broadcasted_iota(jnp.int32, (LANES, 1), 0) + at
            wide = jnp.where(slot < lens[doc], piece[start : start + LANES].astype(F32), 0.0)
            inv = lax.rsqrt(jnp.mean(wide * wide, axis=1, keepdims=True) + EPS)
            normed[rows] = (wide * inv * gain[...].astype(F32)).astype(BF16)
            if sums is not None:
                total = jnp.sum(wide, axis=0, keepdims=True)
                sums[doc : doc + 1] = total if at == 0 else sums[doc : doc + 1] + total
        first += piece.shape[0]
    held_t[...] = normed[...].T
    block = normed_t.shape[0] // len(row_flips)
    for at, flip in enumerate(row_flips):
        start = jnp.bitwise_xor(me[0], flip) * block
        normed_t[at * block : (at + 1) * block] = held_t[pl.ds(pl.multiple_of(start, block), block)]


def factor_rows(normed, w_gate, w_up):
    gate = jnp.dot(normed, w_gate, preferred_element_type=F32)
    up = jnp.dot(normed, w_up, preferred_element_type=F32)
    sig = jax.nn.sigmoid(gate)
    act = gate * sig
    return up * sig * (1.0 + gate * (1.0 - sig)), act, act * up


def own_kernel(row_flips, blocks, me, lens, states, gain, w_gate, w_up, *refs):
    normed_t, sums, held_gate, held_up = refs[:4]
    factors = refs[4 : 4 + 2 * len(blocks)]
    normed, held_t, sems = refs[4 + 2 * len(blocks) :]
    rows, width = states.shape
    hidden_width = held_gate.shape[1]
    docs = lens.shape[0]
    seq = rows // docs
    copies = []
    for at, (start, cols) in enumerate(blocks):
        part = slice(start, start + cols)
        for kind, (w, held) in enumerate(((w_gate, held_gate), (w_up, held_up))):
            copy = pltpu.make_async_copy(w.at[:, part], held.at[:, part], sems.at[kind, at])
            copy.start()
            copies.append(copy)
    norm_rows(
        row_flips, me, lens, [states], gain, normed, normed_t, held_t, sums.at[:, hidden_width : hidden_width + width]
    )
    for doc in range(docs):
        sums[doc : doc + 1, hidden_width + width :] = jnp.full((1, LANES), lens[doc], jnp.int32).astype(F32)
    for at, (start, cols) in enumerate(blocks):
        part = slice(start, start + cols)
        copies[2 * at].wait()
        copies[2 * at + 1].wait()
        for doc in range(docs):
            rows_of = slice(doc * seq, (doc + 1) * seq)
            gate, up, hidden = factor_rows(normed[rows_of], held_gate[:, part], held_up[:, part])
            factors[2 * at][rows_of] = gate.astype(BF16)
            factors[2 * at + 1][rows_of] = up.astype(BF16)
            sums[doc : doc + 1, part] = jnp.sum(hidden.astype(BF16).astype(F32), axis=0, keepdims=True)


def own_call(n_dev, row_flips, blocks, me, lens, states, gain, w_gate, w_up):
    rows, width = states.shape
    hidden_width = w_gate.shape[1]
    docs = lens.shape[0]
    return pl.pallas_call(
        functools.partial(own_kernel, row_flips, blocks),
        out_shape=(
            near_out((width // n_dev * len(row_flips), rows), BF16),
            jax.ShapeDtypeStruct((docs, hidden_width + width + LANES), F32),
            near_out((width, hidden_width), BF16),
            near_out((width, hidden_width), BF16),
        )
        + tuple(near_out((rows, cols), BF16) for _, cols in blocks for _ in range(2)),
        in_specs=[smem(), smem(), vmem(), vmem(), hbm(), hbm()],
        out_specs=(vmem(),) * (4 + 2 * len(blocks)),
        scratch_shapes=[
            pltpu.VMEM((rows, width), BF16),
            pltpu.VMEM((width, rows), BF16),
            pltpu.SemaphoreType.DMA((2, len(blocks))),
        ],
        compiler_params=params(24),
        cost_estimate=cost(),
        name="own_rows",
    )(me, lens, states, gain, far_in(w_gate), far_in(w_up))


def other_kernel(row_flips, pieces, me, lens, gain, w_gate, w_up, *refs):
    states = refs[:pieces]
    normed, normed_t, gate_out, up_out, held_t = refs[pieces:]
    cols = gate_out.shape[1]
    docs = lens.shape[0]
    seq = normed.shape[0] // docs
    norm_rows(row_flips, me, lens, states, gain, normed, normed_t, held_t)
    for doc in range(docs):
        rows_of = slice(doc * seq, (doc + 1) * seq)
        gate, up, _ = factor_rows(normed[rows_of], w_gate[:, :cols], w_up[:, :cols])
        gate_out[rows_of] = gate.astype(BF16)
        up_out[rows_of] = up.astype(BF16)


def other_call(n_dev, row_flips, cols, me, lens, states, gain, w_gate, w_up):
    rows = sum(x.shape[0] for x in states)
    width = states[0].shape[1]
    return pl.pallas_call(
        functools.partial(other_kernel, row_flips, len(states)),
        out_shape=(
            near_out((rows, width), BF16),
            near_out((width // n_dev * len(row_flips), rows), BF16),
            near_out((rows, cols), BF16),
            near_out((rows, cols), BF16),
        ),
        in_specs=[smem(), smem()] + [vmem()] * (3 + len(states)),
        out_specs=(vmem(),) * 4,
        scratch_shapes=[pltpu.VMEM((width, rows), BF16)],
        compiler_params=params(),
        cost_estimate=cost(),
        name="other_rows",
    )(me, lens, gain, near_in(w_gate), near_in(w_up), *states)


def embed_kernel(sums, w_far, rows_out, unit_w, w_down, sems):
    hidden_width, width = w_down.shape
    step = hidden_width // PIECES
    copies = start_pieces(w_far, w_down, sems)
    docs = sums.shape[0]
    hid = sums[:, :hidden_width]
    high = hid.astype(BF16)
    rest = hid - high.astype(F32)
    mid = rest.astype(BF16)
    low = (rest - mid.astype(F32)).astype(BF16)
    split = jnp.concatenate([low.astype(F32), mid.astype(F32), high.astype(F32)], axis=0).astype(BF16)
    total = None
    for at in range(PIECES):
        copies[at].wait()
        part = slice(at * step, (at + 1) * step)
        term = jnp.dot(split[:, part], w_down[part], preferred_element_type=F32)
        total = term if total is None else total + term
    total = total[:docs] + total[docs : 2 * docs] + total[2 * docs :]
    count = sums[:, hidden_width + width : hidden_width + width + 1]
    pooled = (total + sums[:, hidden_width : hidden_width + width]) / count
    inv = lax.rsqrt(jnp.sum(pooled * pooled, axis=1, keepdims=True) + EPS)
    unit = pooled * inv
    embed = unit.astype(BF16).astype(F32)
    rest = unit - embed
    rest_high = rest.astype(BF16).astype(F32)
    stack = jnp.concatenate([embed, rest_high, rest - rest_high], axis=0).astype(BF16)
    product = rows_product(stack, w_down[...])
    unit_w[...] = product[:docs] + (product[docs : 2 * docs] + product[2 * docs :])
    rows_out[:, :hidden_width] = hid
    rows_out[:, hidden_width : hidden_width + width] = unit
    rows_out[:, hidden_width + width : 2 * hidden_width + width] = product[:docs]
    lane = lax.broadcasted_iota(jnp.int32, (docs, LANES), 1)
    rows_out[:, 2 * hidden_width + width :] = jnp.where(lane == 0, count, inv)


def embed_call(sums, w_down):
    hidden_width, width = w_down.shape
    docs = sums.shape[0]
    return pl.pallas_call(
        embed_kernel,
        out_shape=(
            jax.ShapeDtypeStruct((docs, 2 * hidden_width + width + LANES), F32),
            jax.ShapeDtypeStruct((docs, hidden_width), F32),
        ),
        in_specs=[vmem(), hbm()],
        out_specs=(vmem(), vmem()),
        scratch_shapes=[pltpu.VMEM((hidden_width, width), BF16), pltpu.SemaphoreType.DMA((PIECES,))],
        compiler_params=params(),
        cost_estimate=cost(),
        name="embed_rows",
    )(sums, far_in(w_down))


def loss_kernel(
    doc_dev, gather_bits, near_at, me, products, got, rows_a, rows_b, unit_w, loss, d_doc, d_hidden, held
):
    near_docs, hidden_width = unit_w.shape
    docs, width = d_doc.shape
    held[: docs // 2] = rows_a[...]
    held[docs // 2 :] = rows_b[...]
    rows = held[:, hidden_width : hidden_width + width]
    embed_w = held[:, hidden_width + width : 2 * hidden_width + width]
    count = held[:, 2 * hidden_width + width : 2 * hidden_width + width + 1]
    inv = held[:, 2 * hidden_width + width + 1 : 2 * hidden_width + width + 2]
    embed = rows.astype(BF16)
    gram_student = rows_product(embed, embed)
    prod = products[...] + got[...]
    at_row = lax.broadcasted_iota(jnp.int32, (docs, docs), 0)
    at_col = lax.broadcasted_iota(jnp.int32, (docs, docs), 1)
    owner = me[0]
    for place, bit in enumerate(gather_bits):
        owner = jnp.bitwise_xor(owner, jnp.bitwise_and((at_row // doc_dev) >> place, 1) * bit)
    pick = (at_col == owner * doc_dev + at_row % doc_dev).astype(F32)
    prod = jnp.dot(pick, prod, precision=HIGHEST, preferred_element_type=F32)
    prod = rows_product(prod, pick, HIGHEST)
    own = jnp.where(at_row == at_col, prod, 0.0)
    gram_teacher = (
        prod
        * lax.rsqrt(jnp.sum(own, axis=1, keepdims=True) + EPS)
        * lax.rsqrt(jnp.sum(own, axis=0, keepdims=True) + EPS)
    )
    gram_diff = gram_student - gram_teacher
    diff_norm = jnp.sqrt(jnp.sum(gram_diff * gram_diff, keepdims=True) + EPS)
    teacher_norm = jnp.sqrt(jnp.sum(gram_teacher * gram_teacher, keepdims=True))
    loss[...] = jnp.broadcast_to(diff_norm / teacher_norm, loss.shape)
    d_gram = LOSS_SCALE * gram_diff / (diff_norm * teacher_norm)
    d_embed = 2.0 * jnp.dot(d_gram, embed.astype(F32), precision=HIGHEST, preferred_element_type=F32)
    along = jnp.sum(rows * d_embed, axis=1, keepdims=True)
    d_doc[...] = ((d_embed - rows * along) * inv / count).astype(BF16)
    near = lambda x: jnp.concatenate([x[at : at + doc_dev] for at in near_at], axis=0)
    d_embed_w = 2.0 * jnp.dot(near(d_gram), embed_w, precision=HIGHEST, preferred_element_type=F32)
    d_hidden[...] = (d_embed_w - unit_w[...] * near(along)) * near(inv) / near(count)


def loss_call(doc_dev, width, gather_bits, near_at, me, products, got, rows_a, rows_b, unit_w):
    docs = 2 * rows_a.shape[0]
    near, hidden_width = unit_w.shape
    return pl.pallas_call(
        functools.partial(loss_kernel, doc_dev, gather_bits, near_at),
        out_shape=(
            jax.ShapeDtypeStruct((1, LANES), F32),
            jax.ShapeDtypeStruct((docs, width), BF16),
            jax.ShapeDtypeStruct((near, hidden_width), F32),
        ),
        in_specs=[smem()] + [vmem()] * 5,
        out_specs=(vmem(), vmem(), vmem()),
        scratch_shapes=[pltpu.VMEM((docs, rows_a.shape[1]), F32)],
        compiler_params=params(),
        cost_estimate=cost(),
        name="loss_rows",
    )(me, products, got, rows_a, rows_b, unit_w)


def down_kernel(me, rows_a, rows_b, d_doc, grad, held_t):
    docs = d_doc.shape[0]
    hidden_width = held_t.shape[0]
    held_t[:, : docs // 2] = rows_a[:, :hidden_width].T
    held_t[:, docs // 2 : docs] = rows_b[:, :hidden_width].T
    slot = grad.shape[0]
    mine = held_t[pl.ds(pl.multiple_of(me[0] * slot, 8), slot), :docs]
    high = mine.astype(BF16)
    rest = mine - high.astype(F32)
    mid = rest.astype(BF16)
    low = (rest - mid.astype(F32)).astype(BF16)
    right = d_doc[...]
    grad[...] = (
        jnp.dot(low, right, preferred_element_type=F32)
        + jnp.dot(mid, right, preferred_element_type=F32)
        + jnp.dot(high, right, preferred_element_type=F32)
    )


def down_call(n_dev, hidden_width, me, rows_a, rows_b, d_doc):
    docs, width = d_doc.shape
    return pl.pallas_call(
        down_kernel,
        out_shape=jax.ShapeDtypeStruct((hidden_width // n_dev, width), F32),
        in_specs=[smem()] + [vmem()] * 3,
        out_specs=vmem(),
        scratch_shapes=[pltpu.VMEM((hidden_width, max(docs, LANES)), F32)],
        compiler_params=params(),
        cost_estimate=cost(),
        name="down_rows",
    )(me, rows_a, rows_b, d_doc)


def scale_rows(factor, d_hidden, first, docs):
    seq = factor.shape[0] // docs
    parts = [
        (factor[doc * seq : (doc + 1) * seq].astype(F32) * d_hidden[first + doc : first + doc + 1]).astype(BF16)
        for doc in range(docs)
    ]
    return jnp.concatenate(parts, axis=0)


def put_blocks(row_flips, flips_of, outs, place, total):
    block = outs[0].shape[1]
    for out, flips in zip(outs, flips_of):
        for at, flip in enumerate(flips):
            start = row_flips.index(flip) * block
            out[at, :, place] = total[start : start + block].astype(out.dtype)


def first_kernel(docs, shares, row_flips, flips_of, d_hidden, *refs):
    rows_t, factors, outs = refs[:shares], refs[shares : 3 * shares], refs[3 * shares :]
    cols = factors[0].shape[1]
    for part in range(2):
        total = None
        for side in range(shares):
            scaled = scale_rows(factors[2 * side + part], d_hidden[:, :cols], side * docs, docs)
            term = jnp.dot(rows_t[side][...], scaled, preferred_element_type=F32)
            total = term if total is None else total + term
        put_blocks(row_flips, flips_of, outs, slice(part * cols, (part + 1) * cols), total)


def later_kernel(docs, shares, row_flips, flips_of, start, d_hidden, own_gate, own_up, w_gate, w_up, *refs):
    rows_t, normed = refs[:shares], refs[shares : 2 * shares - 1]
    outs = refs[2 * shares - 1 :]
    cols = own_gate.shape[1]
    seq = own_gate.shape[0] // docs
    place = slice(start, start + cols)
    here = d_hidden[:, place]
    totals = [
        jnp.dot(rows_t[0][...], scale_rows(factor, here, 0, docs), preferred_element_type=F32)
        for factor in (own_gate, own_up)
    ]
    for side in range(1, shares):
        for doc in range(docs):
            rows_of = slice(doc * seq, (doc + 1) * seq)
            gate, up, _ = factor_rows(normed[side - 1][rows_of], w_gate[:, place], w_up[:, place])
            at = side * docs + doc
            for part, factor in enumerate((gate, up)):
                scaled = (factor.astype(BF16).astype(F32) * here[at : at + 1]).astype(BF16)
                totals[part] += jnp.dot(rows_t[side][:, rows_of], scaled, preferred_element_type=F32)
    for part in range(2):
        put_blocks(row_flips, flips_of, outs, slice(part * cols, (part + 1) * cols), totals[part])


def block_outs(row_flips, flips_of, height, cols):
    block = height // len(row_flips)
    shape = (len(flips_of[0]), block, 2 * cols)
    return (jax.ShapeDtypeStruct(shape, BF16),) * 2 + (jax.ShapeDtypeStruct(shape, F32),) * 2


def first_call(docs, row_flips, flips_of, d_hidden, rows_t, factors):
    height, rows = rows_t[0].shape
    cols = factors[0].shape[1]
    shares = len(rows_t)
    return pl.pallas_call(
        functools.partial(first_kernel, docs, shares, row_flips, flips_of),
        out_shape=block_outs(row_flips, flips_of, height, cols),
        in_specs=[vmem()] * (1 + 3 * shares),
        out_specs=(vmem(),) * 4,
        compiler_params=params(),
        cost_estimate=cost(),
        name="first_cols",
    )(d_hidden, *[near_in(x) for x in rows_t], *[near_in(x) for x in factors])


def later_call(docs, row_flips, flips_of, start, d_hidden, own_factors, w_gate, w_up, rows_t, normed):
    height, rows = rows_t[0].shape
    cols = own_factors[0].shape[1]
    shares = len(rows_t)
    return pl.pallas_call(
        functools.partial(later_kernel, docs, shares, row_flips, flips_of, start),
        out_shape=block_outs(row_flips, flips_of, height, cols),
        in_specs=[vmem()] * (4 + 2 * shares),
        out_specs=(vmem(),) * 4,
        compiler_params=params(),
        cost_estimate=cost(),
        name="later_cols",
    )(
        d_hidden, *[near_in(x) for x in own_factors], near_in(w_gate), near_in(w_up),
        *[near_in(x) for x in rows_t], *[near_in(x) for x in normed],
    )


def tie(x, *others):
    return lax.optimization_barrier((x,) + others)[0] if others else x


def per_device(
    n_dev, states, lengths, norm_gain, w_gate, w_up, w_down, context, w_out, resid_stream, teacher_gain
):
    doc_dev = lengths.shape[0]
    width, hidden_width = w_gate.shape
    index = lax.axis_index("dp").astype(jnp.int32)
    me = index.reshape(1)
    bits = [1 << k for k in range(n_dev.bit_length() - 1)]
    near = 2
    sum_bits = [b for b in bits if b not in (1, near)]
    gather_bits = [b for b in bits[::-1] if b not in (near, 1)] + [near, 1]

    def span(some):
        flips = [0]
        for bit in some:
            flips = flips + [f ^ bit for f in flips]
        return flips

    row_flips = span(sum_bits)
    gather_flips = span(gather_bits)
    share = (0, near, 1, near ^ 1)
    near_at = [gather_flips.index(f) * doc_dev for f in share]

    def swap(x, flip):
        return lax.ppermute(x, "dp", [(i, i ^ flip) for i in range(n_dev)])

    widths = [hidden_width // 3] * 3
    blocks = [(sum(widths[:k]), w) for k, w in enumerate(widths)]
    gain = norm_gain.reshape(1, width)
    gain_t = teacher_gain.reshape(1, -1)

    teacher_bits = [1] + [b for b in bits if b not in (1, near)] + [near]
    halvings = len(teacher_bits) - 2
    gram_bits = teacher_bits[:halvings][::-1]
    piece = jnp.zeros((), jnp.int32)
    for bit in teacher_bits[:halvings]:
        piece = piece * 2 + jnp.bitwise_and(index // bit, 1)
    piece = piece.reshape(1)
    send, attn = arrange_call(1 << halvings, piece, near_in(jnp.dot(context, w_out, preferred_element_type=F32)))

    lens_of = {0: lengths, near: swap(lengths, near), 1: swap(lengths, 1)}
    states_of = {near: [swap(states, near)], 1: [swap(states, 1)]}
    lens_of[near ^ 1] = swap(lens_of[near], 1)
    normed_of, rows_t, factors = {}, {}, {}
    state = {}

    def other(flip, *after):
        normed_of[flip], rows_t[flip], *factors[flip] = other_call(
            n_dev, row_flips, widths[0], me, lens_of[flip], [tie(x, *after) for x in states_of[flip]], gain,
            *state["weights"],
        )
        return rows_t[flip]

    def gather_step(after):
        if state["bits"]:
            bit = state["bits"].pop(0)
            if "got" in state:
                state["rows"] = jnp.concatenate([state["rows"], state["got"]], axis=0)
            state["rows"] = tie(state["rows"], after)
            state["got"] = swap(state["rows"], bit)
            if bit in (near, 1):
                mine = tie(state["unit_w"], after)
                state["unit_w"] = jnp.concatenate([mine, swap(mine, bit)], axis=0)

    def beside(step, after):
        if step < halvings:
            return ()
        if step == halvings:
            rows_t[0], sums, *rest = own_call(
                n_dev, row_flips, blocks, me, lengths, tie(states, after), gain, w_gate, w_up
            )
            state["weights"], factors[0] = rest[:2], rest[2:]
            state["sums"] = sums
            return (sums,)
        gather_step(after)
        if step == halvings + 1:
            return (other(1, after),)
        if step == halvings + 2:
            states_of[near ^ 1] = [swap(tie(x, after), 1) for x in states_of[near]]
            return (other(near, after),)
        if step == halvings + 3:
            return (other(near ^ 1, after),)
        return ()

    before = ()
    for step, bit in enumerate(teacher_bits):
        if step < halvings:
            send = tie(send, *before)
            before = beside(step, send)
            got = swap(send, bit)
            if step + 1 < halvings:
                send, attn = fold_call(attn, got)
            else:
                attn = fold_last_call(attn, got)
        else:
            attn = tie(attn, *before)
            before = beside(step, attn)
            got = swap(attn, bit)
            if step == halvings:
                attn = fold_last_call(attn, got)
                state["rows"], state["unit_w"] = embed_call(tie(state["sums"], attn), w_down)
                state["bits"] = list(gather_bits)
                for _ in range(len(bits) - 2):
                    gather_step(attn)
                before = (state["rows"], *states_of[near])
    products = gram_call(piece, attn, got, resid_stream, gain_t)
    for step, bit in enumerate(gram_bits):
        products = tie(products, *before) if step == 0 else tie(products + got, *before)
        before = beside(len(bits) + step, products)
        got = swap(products, bit)
    while state["bits"]:
        gather_step(products)
    loss, d_doc, d_hidden = loss_call(
        doc_dev, width, gather_bits, near_at, me, tie(products, *before), got, state["rows"], state["got"],
        state["unit_w"],
    )

    order = sum_bits
    first_flips = [f for f in row_flips if f & order[0]]
    key = lambda f: tuple(-((f & b) != 0) for b in order[2:])
    sent_on = sorted([f for f in first_flips if f & order[1]], key=key)
    sent_end = [f ^ order[1] for f in sent_on]
    flips_of = (sent_on, sent_end, [f ^ order[0] for f in sent_on], [f ^ order[0] for f in sent_end])
    results = []
    arrived = []
    passed = []
    all_rows = [rows_t[f] for f in share]
    for at, (start, cols) in enumerate(blocks):
        if at == 0:
            firsts = list(factors[0][:2])
            for flip in share[1:]:
                firsts += factors[flip]
            outs = first_call(doc_dev, row_flips, flips_of, d_hidden, all_rows, firsts)
        else:
            outs = later_call(
                doc_dev, row_flips, flips_of, start, tie(d_hidden, outs[0], *[g for pair in arrived[: at - 1] for g in pair]),
                factors[0][2 * at : 2 * at + 2], *state["weights"], all_rows, [normed_of[f] for f in share[1:]],
            )
        sent_a, sent_b, kept_a, kept_b = outs
        if at == len(blocks) - 1:
            sent_a = tie(sent_a, *arrived[-1], *passed[:1])
        got_a, got_b = swap(sent_a, order[0]), swap(sent_b, order[0])
        arrived.append((got_a, got_b))
        part = (kept_a + got_a.astype(F32)).astype(BF16)
        kept = kept_b + got_b.astype(F32)
        for step in order[1:]:
            got = swap(part, step)
            passed.append(got)
            half = got.shape[0] // 2
            if half:
                part = (kept[:half] + got[:half].astype(F32)).astype(BF16)
                kept = kept[half:] + got[half:].astype(F32)
            else:
                kept = kept + got.astype(F32)
        results.append(kept[0])
    grad_gate = jnp.concatenate([r[:, :cols] for r, (_, cols) in zip(results, blocks)], axis=1)
    grad_up = jnp.concatenate([r[:, cols:] for r, (_, cols) in zip(results, blocks)], axis=1)

    grad_down = down_call(n_dev, hidden_width, me, state["rows"], state["got"], d_doc)
    return (loss[0, :1], grad_gate, grad_up, grad_down)


def solution(mesh):
    in_specs = (
        P(("groups", "dp"), None),
        P(("groups", "dp")),
        P(),
        P(),
        P(),
        P(),
        P("groups", "dp"),
        P("dp", None),
        P("groups", None),
        P(),
    )
    out_specs = (
        P("groups"),
        P(("groups", "dp"), None),
        P(("groups", "dp"), None),
        P(("groups", "dp"), None),
    )
    return jax.shard_map(
        functools.partial(per_device, mesh.shape["dp"]),
        mesh=mesh,
        in_specs=in_specs,
        out_specs=out_specs,
        check_vma=False,
    )
```
